32 devices in a mesh: group: 2 (over x), seq: 16 (over z, y, core).
Axes of the slice: x: 2, y: 2, z: 4, core: 2. Of those that a mesh axis runs over, the one named last changes fastest.
Arguments:
- query: bfloat16 [12288, 1536], P(('group', 'seq')), parts along dimension 0, may hold values from -32 to 32
- keys_values: bfloat16 [12288, 3072], P(('group', 'seq')), parts along dimension 0, may hold values from -32 to 32
- dout: bfloat16 [12288, 1536], P(('group', 'seq')), parts along dimension 0, may hold values from -6 to 6
- lengths: int32 [8], P('group'), parts along dimension 0, may hold values from 1 to 3072, 6144 in all
- latent_kv: bfloat16 [512, 3072], P(('group', 'seq')), parts along dimension 0, may hold values from -6 to 6
Outputs:
- grad_query: bfloat16 [12288, 1536], P(('group', 'seq')), parts along dimension 0
- grad_kv: bfloat16 [12288, 3072], P(('group', 'seq')), parts along dimension 0
- grad_latent: bfloat16 [512, 3072], P(('group', 'seq')), parts along dimension 0
The draws below stay inside these ranges and needn't reach their ends.
There are 2 independent parts, one for each index of `group`. The reference program is written for one: setup_inputs(seed, part) draws one part's arguments, and reference() takes and returns one part's arrays. A program takes and returns all parts, laid end to end along the dimension named above; each array names one. Nothing has to cross between parts.
Inputs may be any that keep to these rules, and one draw needn't show every extreme that they name: `lengths`: they sum to 6144 and the longest mesh has exactly 3072 tokens.
All inputs are finite; a program needn't handle non-finite values.
Results may differ from the reference program's by a relative error of at most 0.0092.
Values may be sent and summed in bfloat16 or wider, within the bound.
A program may use at most 128 MiB of HBM per device.

```python
import math
import jax
import jax.numpy as jnp
import numpy as np
from jax import lax

H = 12
DH = 128
WIN = 768
TOK_DEV = 384
MESHES = 4
TOKENS = 6144
LATS = 256
N_SEQ = 16


def draw_query(key, part):
    fresh = jax.random.truncated_normal(jax.random.fold_in(key, 5), -4.0, 4.0, (TOKENS, H * DH), jnp.float32)
    return fresh.astype(jnp.bfloat16)


def draw_keys_values(key, part):
    fresh = jax.random.truncated_normal(jax.random.fold_in(key, 6), -4.0, 4.0, (TOKENS, 2 * H * DH), jnp.float32)
    return fresh.astype(jnp.bfloat16)


def level_of(own_key, shape, shards, smallest, high):
    loudness, own = 1.0, jax.random.fold_in(own_key, 6)
    for position, blocks in shards:
        steps = jnp.exp(jax.random.uniform(jax.random.fold_in(own, position), (blocks,), jnp.float32, smallest / len(shards), high / len(shards)))
        loudness = loudness * jnp.repeat(steps, shape[position] // blocks).reshape([-1 if axis == position else 1 for axis in range(len(shape))])
    return loudness


def profile(amount, total, most, skew):
    weights = [(1 << 20) // math.isqrt(rank ** skew) + 1 for rank in range(2, amount + 1)]
    surplus, counts = total - most - (amount - 1), [1] * (amount - 1)
    while surplus > 0:
        movable = [i for i in range(amount - 1) if counts[i] < most]
        pool, budget = sum([weights[i] for i in movable]), surplus
        for i in movable:
            extra = min(most - counts[i], max(1, budget * weights[i] // pool), surplus)
            counts[i] = counts[i] + extra
            surplus = surplus - extra
    return np.array([most] + counts)


def uneven(key, number_of, total, most, lean):
    if number_of == 2:
        one = jax.random.randint(key, (), max(1, total - most), min(most, total - 1) + 1)
        return jnp.stack([one, total - one])
    tallies = jnp.asarray(profile(number_of, total, most, lean), jnp.int32)
    couples = (number_of - 1) // 2
    giver, taker = tallies[1:1 + 2 * couples:2], tallies[2:2 + 2 * couples:2]
    slack = jnp.minimum(giver - 1, most - taker)
    shifted = jax.random.randint(jax.random.fold_in(key, 1), (couples,), 0, 1 << 20) % (slack + 1)
    tallies = tallies.at[1:1 + 2 * couples:2].set(giver - shifted).at[2:2 + 2 * couples:2].set(taker + shifted)
    return tallies[jax.random.permutation(jax.random.fold_in(key, 2), number_of)]


def normal_values(rng, shape, deviation, limit, pieces=(), kind=jnp.bfloat16):
    loudness = level_of(rng, shape, pieces, -0.22, 0.18) if pieces else 1.0
    entries = jax.random.normal(rng, shape, jnp.float32) * deviation * loudness
    return jnp.minimum(jnp.maximum(entries, -limit), limit).astype(kind)


def setup_inputs(seed: int = 0, part: int = 0) -> dict:
    splits = jax.random.split(jax.random.key(seed), 6)
    part_keys = jax.random.split(jax.random.fold_in(splits[5], part), 6)
    return {
        "query": draw_query(jax.random.fold_in(jax.random.fold_in(splits[5], part), 71), part),
        "keys_values": draw_keys_values(jax.random.fold_in(jax.random.fold_in(splits[5], part), 71), part),
        "dout": normal_values(part_keys[2], (TOKENS, H * DH), 1.0, 6.0, ((0, 16),)),
        "lengths": uneven(part_keys[3], MESHES, TOKENS, TOKENS // 2, 2).astype(jnp.int32),
        "latent_kv": normal_values(part_keys[4], (LATS, 2 * H * DH), 1.0, 6.0, ((0, 16),)),
    }


def segment_index(positions, mesh_ends):
    return lax.optimization_barrier(jnp.sum((positions[:, None] >= mesh_ends[None, :]).astype(jnp.int32), axis=1))

def dot_float(left, right):
    return jnp.dot(left.astype(jnp.float32), right.astype(jnp.float32), preferred_element_type=jnp.float32)

def head_grads(q_head, k_win, v_win, k_lat, v_lat, do_head, window_mask, latent_mask, score_scale):
    score_win = jnp.where(window_mask, dot_float(q_head, k_win.T) * score_scale, -1e+30)
    score_lat = jnp.where(latent_mask, dot_float(q_head, k_lat.T) * score_scale, -1e+30)
    row_max = jnp.maximum(lax.optimization_barrier(jnp.max(score_win, axis=1, keepdims=True)), lax.optimization_barrier(jnp.max(score_lat, axis=1, keepdims=True)))
    exp_win = jnp.where(window_mask, jnp.exp(score_win - row_max), 0.0)
    exp_lat = jnp.where(latent_mask, jnp.exp(score_lat - row_max), 0.0)
    row_sum = lax.optimization_barrier(jnp.sum(exp_win, axis=1, keepdims=True)) + lax.optimization_barrier(jnp.sum(exp_lat, axis=1, keepdims=True))
    prob_win = exp_win / row_sum
    prob_lat = exp_lat / row_sum
    rounded_win = prob_win.astype(jnp.bfloat16)
    rounded_lat = prob_lat.astype(jnp.bfloat16)
    attended = dot_float(rounded_win, v_win) + dot_float(rounded_lat, v_lat)
    dprob_win = dot_float(do_head, v_win.T)
    dprob_lat = dot_float(do_head, v_lat.T)
    row_delta = lax.optimization_barrier(jnp.sum(do_head.astype(jnp.float32) * attended, axis=1, keepdims=True))
    dscore_win = (prob_win * (dprob_win - row_delta)).astype(jnp.bfloat16)
    dscore_lat = (prob_lat * (dprob_lat - row_delta)).astype(jnp.bfloat16)
    grad_q = (dot_float(dscore_win, k_win) + dot_float(dscore_lat, k_lat)) * score_scale
    grad_k = dot_float(dscore_win.T, q_head) * score_scale
    grad_v = dot_float(rounded_win.T, do_head)
    grad_lk = dot_float(dscore_lat.T, q_head) * score_scale
    grad_lv = dot_float(rounded_lat.T, do_head)
    return (grad_q, grad_k, grad_v, grad_lk, grad_lv)

def reference(query, keys_values, dout, lengths, latent_kv):
    model_width = H * DH
    score_scale = 1.0 / math.sqrt(DH)
    mesh_ends = jnp.cumsum(lengths).astype(jnp.int32)
    latent_seg = jnp.arange(LATS, dtype=jnp.int32) % MESHES
    padded = jnp.concatenate([jnp.zeros((WIN, 2 * model_width), keys_values.dtype), keys_values], axis=0)

    def split_heads(block):
        return block.reshape(block.shape[0], H, DH).transpose(1, 0, 2)

    def merge_heads(part):
        return part.transpose(1, 0, 2).reshape(part.shape[1], model_width)
    lat_keys = split_heads(latent_kv[:, :model_width])
    lat_vals = split_heads(latent_kv[:, model_width:])

    def one_block(totals, block_idx):
        grad_kv, grad_lat = totals
        row_start = (block_idx * TOK_DEV).astype(jnp.int32)
        q_blk = lax.dynamic_slice_in_dim(query, row_start, TOK_DEV, 0)
        do_blk = lax.dynamic_slice_in_dim(dout, row_start, TOK_DEV, 0)
        kv_blk = lax.dynamic_slice_in_dim(padded, row_start, WIN + TOK_DEV, 0)
        query_pos = row_start + jnp.arange(TOK_DEV, dtype=jnp.int32)
        key_pos = row_start - WIN + jnp.arange(WIN + TOK_DEV, dtype=jnp.int32)
        query_seg = segment_index(query_pos, mesh_ends)
        key_seg = segment_index(key_pos, mesh_ends)
        window_mask = (key_pos[None, :] > query_pos[:, None] - WIN) & (key_pos[None, :] <= query_pos[:, None]) & (key_pos[None, :] >= 0) & (key_seg[None, :] == query_seg[:, None])
        latent_mask = latent_seg[None, :] == query_seg[:, None]

        def per_head(parts):
            return head_grads(parts[0], parts[1], parts[2], parts[3], parts[4], parts[5], window_mask, latent_mask, score_scale)
        grad_q, grad_k, grad_v, grad_lk, grad_lv = lax.map(per_head, (split_heads(q_blk), split_heads(kv_blk[:, :model_width]), split_heads(kv_blk[:, model_width:]), lat_keys, lat_vals, split_heads(do_blk)))
        dq_blk = merge_heads(grad_q).astype(jnp.bfloat16)
        contrib = jnp.concatenate([merge_heads(grad_k).astype(jnp.bfloat16), merge_heads(grad_v).astype(jnp.bfloat16)], axis=1).astype(jnp.float32)
        current = lax.dynamic_slice_in_dim(grad_kv, row_start, WIN + TOK_DEV, 0)
        grad_kv = lax.dynamic_update_slice_in_dim(grad_kv, current + contrib, row_start, 0)
        grad_lat = grad_lat + jnp.concatenate([merge_heads(grad_lk), merge_heads(grad_lv)], axis=1)
        return ((grad_kv, grad_lat), dq_blk)
    start_totals = (jnp.zeros((WIN + TOKENS, 2 * model_width), jnp.float32), jnp.zeros((LATS, 2 * model_width), jnp.float32))
    (grad_kv, grad_lat), dq_blocks = lax.scan(one_block, start_totals, jnp.arange(N_SEQ, dtype=jnp.int32))
    return (dq_blocks.reshape(TOKENS, model_width), grad_kv[WIN:].astype(jnp.bfloat16), grad_lat.astype(jnp.bfloat16))
```

```python
import functools
import math

import jax
import jax.numpy as jnp
from jax import lax
from jax.experimental import pallas as pl
from jax.experimental.pallas import tpu as pltpu
from jax.sharding import PartitionSpec as P

DH = 128
MESHES = 4
PER = 2
MESH = pl.DeviceIdType.MESH
NT = (((1,), (1,)), ((), ()))
NN = (((1,), (0,)), ((), ()))
TN = (((0,), (0,)), ((), ()))


def dot(a, b, dims):
    return lax.dot_general(a, b, dims, preferred_element_type=jnp.float32)


def kernel(
    n, q, kv, do, lengths, lat, dq, dkv, dlat,
    far, mid, back, near, near_in, far_in, bias_c, bias_m, bias_l,
    s_far, r_far, s_mid, r_mid, s_near, r_near, s_back, r_back,
):
    me = lax.axis_index("seq")
    core = lax.rem(me, 2)
    partner = me + 1 - 2 * core
    ahead, behind = lax.rem(me + 2, n), lax.rem(me + n - 2, n)
    rows, width = q.shape
    lats = lat.shape[0]
    groups = width // (PER * DH)
    scale = 1.0 / math.sqrt(DH)
    has_ahead, has_behind = me + 2 < n, me >= 2

    barrier = pltpu.get_barrier_semaphore()
    for other in (partner, ahead, behind):
        pl.semaphore_signal(barrier, inc=1, device_id={"seq": other}, device_id_type=MESH)
    pl.semaphore_wait(barrier, 3)

    def cols(g, s):
        return pl.ds(pl.multiple_of(s * width + g * (PER * DH), DH), PER * DH)

    def copy(src, dst, send, recv, to, g, s):
        return pltpu.make_async_remote_copy(
            src_ref=src.at[:, cols(g, s)], dst_ref=dst.at[:, cols(g, s)],
            send_sem=send.at[g, s], recv_sem=recv.at[g, s],
            device_id={"seq": to}, device_id_type=MESH,
        )

    def far_copy(g, s):
        return copy(kv, far, s_far, r_far, ahead, g, s)

    def mid_copy(src, g, s):
        return copy(src, mid, s_mid, r_mid, partner, g, s)

    def near_copy(g, s):
        return copy(near, near_in, s_near, r_near, partner, g, s)

    def back_copy(g, s):
        return copy(back, far_in, s_back, r_back, behind, g, s)

    def each(fn):
        def step(g, carry):
            for s in (0, 1):
                fn(g, s)
            return carry

        lax.fori_loop(0, groups, step, 0)

    @pl.when(has_ahead)
    def _():
        each(lambda g, s: far_copy(g, s).start())

    @pl.when(core == 0)
    def _():
        each(lambda g, s: mid_copy(kv, g, s).start())

    @pl.when(jnp.logical_not(has_behind))
    def _():
        far[...] = jnp.zeros_like(far)

    ends = []
    total = jnp.int32(0)
    for k in range(MESHES):
        total = total + lengths[k]
        ends.append(total)

    def seg(pos):
        out = jnp.zeros(pos.shape, jnp.int32)
        for e in ends:
            out = out + jnp.where(pos >= e, 1, 0)
        return out

    key = lax.broadcasted_iota(jnp.int32, (rows, rows), 0)
    qry = lax.broadcasted_iota(jnp.int32, (rows, rows), 1)
    q_seg = seg(me * rows + qry)
    pos_c = me * rows + key - jnp.where(key > qry, 2 * rows, 0)
    bias_c[...] = jnp.where((seg(pos_c) == q_seg) & (pos_c >= 0), 0.0, -1e30)
    pos_m = (me - 1) * rows + key
    bias_m[...] = jnp.where((seg(pos_m) == q_seg) & (pos_m >= 0), 0.0, -1e30)
    l_key = lax.broadcasted_iota(jnp.int32, (lats, rows), 0)
    l_qry = lax.broadcasted_iota(jnp.int32, (lats, rows), 1)
    bias_l[...] = jnp.where(lax.rem(l_key, MESHES) == seg(me * rows + l_qry), 0.0, -1e30)

    def head(h):
        kc = pl.ds(pl.multiple_of(h * DH, DH), DH)
        vc = pl.ds(pl.multiple_of(width + h * DH, DH), DH)
        tri = lax.broadcasted_iota(jnp.int32, (rows, rows), 0) > lax.broadcasted_iota(
            jnp.int32, (rows, rows), 1
        )
        qh, doh = q[:, kc], do[:, kc]
        k_f, k_o, k_m, k_l = far[:, kc], kv[:, kc], mid[:, kc], lat[:, kc]
        v_f, v_o, v_m, v_l = far[:, vc], kv[:, vc], mid[:, vc], lat[:, vc]
        c = scale * math.log2(math.e)
        t_c = jnp.where(tri, dot(k_f, qh, NT), dot(k_o, qh, NT)) * c + bias_c[...]
        t_m = dot(k_m, qh, NT) * c + bias_m[...]
        t_l = dot(k_l, qh, NT) * c + bias_l[...]
        top = jnp.maximum(
            jnp.maximum(jnp.max(t_c, axis=0, keepdims=True), jnp.max(t_m, axis=0, keepdims=True)),
            jnp.max(t_l, axis=0, keepdims=True),
        )
        e_c, e_m, e_l = jnp.exp2(t_c - top), jnp.exp2(t_m - top), jnp.exp2(t_l - top)
        inv = 1.0 / (
            jnp.sum(e_c, axis=0, keepdims=True)
            + jnp.sum(e_m, axis=0, keepdims=True)
            + jnp.sum(e_l, axis=0, keepdims=True)
        )
        p_c, p_m, p_l = e_c * inv, e_m * inv, e_l * inv
        b_c, b_m, b_l = (p.astype(jnp.bfloat16) for p in (p_c, p_m, p_l))
        d_c = jnp.where(tri, dot(v_f, doh, NT), dot(v_o, doh, NT))
        d_m, d_l = dot(v_m, doh, NT), dot(v_l, doh, NT)
        delta = (
            jnp.sum(b_c.astype(jnp.float32) * d_c, axis=0, keepdims=True)
            + jnp.sum(b_m.astype(jnp.float32) * d_m, axis=0, keepdims=True)
            + jnp.sum(b_l.astype(jnp.float32) * d_l, axis=0, keepdims=True)
        )
        g_c = p_c * (d_c - delta)
        g_f = jnp.where(tri, g_c, 0.0).astype(jnp.bfloat16)
        g_o = jnp.where(tri, 0.0, g_c).astype(jnp.bfloat16)
        g_m = (p_m * (d_m - delta)).astype(jnp.bfloat16)
        g_l = (p_l * (d_l - delta)).astype(jnp.bfloat16)
        b_f = jnp.where(tri, p_c, 0.0).astype(jnp.bfloat16)
        b_o = jnp.where(tri, 0.0, p_c).astype(jnp.bfloat16)
        back[:, kc] = (dot(g_f, qh, NN) * scale).astype(jnp.bfloat16)
        back[:, vc] = dot(b_f, doh, NN).astype(jnp.bfloat16)
        near[:, kc] = (dot(g_m, qh, NN) * scale).astype(jnp.bfloat16)
        near[:, vc] = dot(b_m, doh, NN).astype(jnp.bfloat16)
        dkv[:, kc] = (dot(g_o, qh, NN) * scale).astype(jnp.bfloat16)
        dkv[:, vc] = dot(b_o, doh, NN).astype(jnp.bfloat16)
        dlat[:, kc] = dot(g_l, qh, NN) * scale
        dlat[:, vc] = dot(b_l, doh, NN)
        dq_t = dot(k_f, g_f, TN) + dot(k_o, g_o, TN) + dot(k_m, g_m, TN) + dot(k_l, g_l, TN)
        dq[:, kc] = (jnp.transpose(dq_t) * scale).astype(jnp.bfloat16)

    def join_and_send(g):
        for s in (0, 1):
            near_copy(g, s).wait_recv()
            w = cols(g, s)
            back[:, w] = (back[:, w].astype(jnp.float32) + near_in[:, w].astype(jnp.float32)).astype(
                jnp.bfloat16
            )

            @pl.when(has_behind)
            def _(s=s):
                back_copy(g, s).start()

    def group(g, carry):
        @pl.when(has_behind)
        def _():
            for s in (0, 1):
                far_copy(g, s).wait_recv()

        @pl.when(core == 1)
        def _():
            for s in (0, 1):
                mid_copy(far, g, s).start()

        for s in (0, 1):
            mid_copy(kv, g, s).wait_recv()
        for i in range(PER):
            head(g * PER + i)
        for s in (0, 1):
            near_copy(g, s).start()

        @pl.when((core == 0) & has_behind)
        def _():
            for s in (0, 1):
                back_copy(g, s).start()

        @pl.when((core == 1) & (g > 0))
        def _():
            join_and_send(g - 1)

        return carry

    lax.fori_loop(0, groups, group, 0)

    @pl.when(core == 1)
    def _():
        join_and_send(groups - 1)

    def add_in(ref, g, s):
        w = cols(g, s)
        dkv[:, w] = (dkv[:, w].astype(jnp.float32) + ref[:, w].astype(jnp.float32)).astype(jnp.bfloat16)

    def finish(g, s):
        w = cols(g, s)
        near_copy(g, s).wait_recv()
        back_copy(g, s).wait_recv()
        dkv[:, w] = (
            dkv[:, w].astype(jnp.float32) + near_in[:, w].astype(jnp.float32) + far_in[:, w].astype(jnp.float32)
        ).astype(jnp.bfloat16)

    def finish_odd(g, s):
        back_copy(g, s).wait_recv()
        add_in(far_in, g, s)

    def finish_last(g, s):
        near_copy(g, s).wait_recv()
        add_in(near_in, g, s)

    @pl.when((core == 0) & has_ahead)
    def _():
        each(finish)

    @pl.when((core == 1) & has_ahead)
    def _():
        each(finish_odd)

    @pl.when((core == 0) & jnp.logical_not(has_ahead))
    def _():
        each(finish_last)

    def sent(g, s):
        mid_copy(kv, g, s).wait_send()
        near_copy(g, s).wait_send()

    each(sent)

    @pl.when(has_ahead)
    def _():
        each(lambda g, s: far_copy(g, s).wait_send())

    @pl.when(has_behind)
    def _():
        each(lambda g, s: back_copy(g, s).wait_send())


def shards(query, keys_values, dout, lengths, latent_kv):
    n = lax.axis_size("seq")
    rows, width = query.shape
    groups = width // (PER * DH)
    latents = lax.all_gather(latent_kv, "seq", axis=0, tiled=True)
    lats = latents.shape[0]
    vmem = pl.BlockSpec(memory_space=pltpu.VMEM)
    wide = pltpu.VMEM((rows, 2 * width), jnp.bfloat16)
    sem = pltpu.SemaphoreType.DMA((groups, 2))
    grad_query, grad_kv, terms = pl.pallas_call(
        functools.partial(kernel, n),
        out_shape=(
            jax.ShapeDtypeStruct((rows, width), jnp.bfloat16),
            jax.ShapeDtypeStruct((rows, 2 * width), jnp.bfloat16),
            jax.ShapeDtypeStruct((lats, 2 * width), jnp.float32),
        ),
        in_specs=[vmem, vmem, vmem, pl.BlockSpec(memory_space=pltpu.SMEM), vmem],
        out_specs=(vmem, vmem, vmem),
        scratch_shapes=[wide] * 6
        + [
            pltpu.VMEM((rows, rows), jnp.float32),
            pltpu.VMEM((rows, rows), jnp.float32),
            pltpu.VMEM((lats, rows), jnp.float32),
        ]
        + [sem] * 8,
        compiler_params=pltpu.CompilerParams(
            collective_id=0, has_side_effects=True, vmem_limit_bytes=56 << 20
        ),
    )(query, keys_values, dout, lengths, latents)
    grad_latent = lax.psum_scatter(terms, "seq", scatter_dimension=0, tiled=True)
    return grad_query, grad_kv, grad_latent.astype(jnp.bfloat16)


def solution(mesh):
    split = P(("group", "seq"), None)
    return jax.shard_map(
        shards,
        mesh=mesh,
        in_specs=(split, split, split, P("group"), split),
        out_specs=(split, split, split),
        check_vma=False,
    )
```

```python
import functools
import math

import jax
import jax.numpy as jnp
from jax import lax
from jax.experimental import pallas as pl
from jax.experimental.pallas import tpu as pltpu
from jax.sharding import PartitionSpec as P

DH = 128
MESHES = 4
PER = 2
MESH = pl.DeviceIdType.MESH
NT = (((1,), (1,)), ((), ()))
NN = (((1,), (0,)), ((), ()))
TN = (((0,), (0,)), ((), ()))


def dot(a, b, dims):
    return lax.dot_general(a, b, dims, preferred_element_type=jnp.float32)


def kernel(
    n, inside, q, kv, do, lengths, lat_in, dq, dkv, dlat_out,
    far, mid, back, near, near_in, far_in, bias_c, bias_m, bias_l,
    s_far, r_far, s_mid, r_mid, s_near, r_near, s_back, r_back, *more,
):
    if inside:
        lat, dlat, half_out, half_in, half_sum, terms = more[:6]
        s_lat, r_lat, s_swap, r_swap, s_half, r_half, s_term, r_term = more[6:]
    else:
        lat, dlat = lat_in, dlat_out
    me = lax.axis_index("seq")
    core = lax.rem(me, 2)
    partner = me + 1 - 2 * core
    ahead, behind = lax.rem(me + 2, n), lax.rem(me + n - 2, n)
    rows, width = q.shape
    lats = lat.shape[0]
    half = lats // 2
    groups = width // (PER * DH)
    scale = 1.0 / math.sqrt(DH)
    has_ahead, has_behind = me + 2 < n, me >= 2

    barrier = pltpu.get_barrier_semaphore()
    chips = n // 2
    chip = me // 2

    def onward(i):
        return lax.rem(chip + i, chips) * 2 + core

    greeted = [partner] + ([onward(i) for i in range(1, chips)] if inside else [ahead, behind])
    for other in greeted:
        pl.semaphore_signal(barrier, inc=1, device_id={"seq": other}, device_id_type=MESH)
    pl.semaphore_wait(barrier, len(greeted))

    def cols(g, s):
        return pl.ds(pl.multiple_of(s * width + g * (PER * DH), DH), PER * DH)

    def copy(src, dst, send, recv, to, g, s):
        return pltpu.make_async_remote_copy(
            src_ref=src.at[:, cols(g, s)], dst_ref=dst.at[:, cols(g, s)],
            send_sem=send.at[g, s], recv_sem=recv.at[g, s],
            device_id={"seq": to}, device_id_type=MESH,
        )

    def far_copy(g, s):
        return copy(kv, far, s_far, r_far, ahead, g, s)

    def mid_copy(src, g, s):
        return copy(src, mid, s_mid, r_mid, partner, g, s)

    def near_copy(g, s):
        return copy(near, near_in, s_near, r_near, partner, g, s)

    def back_copy(g, s):
        return copy(back, far_in, s_back, r_back, behind, g, s)

    def each(fn):
        def step(g, carry):
            for s in (0, 1):
                fn(g, s)
            return carry

        lax.fori_loop(0, groups, step, 0)

    if inside:
        own = lat_in.shape[0]
        half = chips * own

        def rows_of(c, k):
            return pl.ds(pl.multiple_of(c * half + k * own, 16), own)

        def lat_copy(i):
            here = rows_of(core, chip)
            return pltpu.make_async_remote_copy(
                src_ref=lat_in, dst_ref=lat.at[here], send_sem=s_lat.at[i], recv_sem=r_lat.at[i],
                device_id={"seq": onward(i)}, device_id_type=MESH,
            )

        def swap_copy(i):
            at = rows_of(core, lax.rem(chip + chips - i, chips))
            return pltpu.make_async_remote_copy(
                src_ref=lat_in if isinstance(i, int) else lat.at[at], dst_ref=lat.at[at],
                send_sem=s_swap.at[i], recv_sem=r_swap.at[i],
                device_id={"seq": partner}, device_id_type=MESH,
            )

        def half_copy(g, s):
            return copy(half_out, half_in, s_half, r_half, partner, g, s)

        batches = s_term.shape[0]
        span = width // batches

        def term_copy(b, s, i):
            w = pl.ds(pl.multiple_of(s * width + b * span, DH), span)
            to = pl.ds(pl.multiple_of(lax.rem(chip + i, chips) * own, 16), own)
            slot = pl.ds(pl.multiple_of(chip * own, 16), own)
            return pltpu.make_async_remote_copy(
                src_ref=half_sum.at[to, w], dst_ref=terms.at[slot, w],
                send_sem=s_term.at[b, s, i], recv_sem=r_term.at[b, s, i],
                device_id={"seq": onward(i)}, device_id_type=MESH,
            )

        def chips_on(fn):
            lax.fori_loop(1, chips, lambda i, c: (fn(i), c)[1], 0)

        chips_on(lambda i: lat_copy(i).start())
        swap_copy(0).start()
        lat[rows_of(core, chip), :] = lat_in[...]

    @pl.when(has_ahead)
    def _():
        each(lambda g, s: far_copy(g, s).start())

    @pl.when(core == 0)
    def _():
        each(lambda g, s: mid_copy(kv, g, s).start())

    @pl.when(jnp.logical_not(has_behind))
    def _():
        far[...] = jnp.zeros_like(far)

    ends = []
    total = jnp.int32(0)
    for k in range(MESHES):
        total = total + lengths[k]
        ends.append(total)

    def seg(pos):
        out = jnp.zeros(pos.shape, jnp.int32)
        for e in ends:
            out = out + jnp.where(pos >= e, 1, 0)
        return out

    key = lax.broadcasted_iota(jnp.int32, (rows, rows), 0)
    qry = lax.broadcasted_iota(jnp.int32, (rows, rows), 1)
    q_seg = seg(me * rows + qry)
    pos_c = me * rows + key - jnp.where(key > qry, 2 * rows, 0)
    bias_c[...] = jnp.where((seg(pos_c) == q_seg) & (pos_c >= 0), 0.0, -1e30)
    pos_m = (me - 1) * rows + key
    bias_m[...] = jnp.where((seg(pos_m) == q_seg) & (pos_m >= 0), 0.0, -1e30)
    l_key = lax.broadcasted_iota(jnp.int32, (lats, rows), 0)
    l_qry = lax.broadcasted_iota(jnp.int32, (lats, rows), 1)
    bias_l[...] = jnp.where(lax.rem(l_key, MESHES) == seg(me * rows + l_qry), 0.0, -1e30)

    if inside:

        def forward(i):
            lat_copy(i).wait_recv()
            swap_copy(i).start()

        chips_on(forward)
        swap_copy(0).wait_recv()
        chips_on(lambda i: swap_copy(i).wait_recv())

    def head(h):
        kc = pl.ds(pl.multiple_of(h * DH, DH), DH)
        vc = pl.ds(pl.multiple_of(width + h * DH, DH), DH)
        tri = lax.broadcasted_iota(jnp.int32, (rows, rows), 0) > lax.broadcasted_iota(
            jnp.int32, (rows, rows), 1
        )
        qh, doh = q[:, kc], do[:, kc]
        k_f, k_o, k_m, k_l = far[:, kc], kv[:, kc], mid[:, kc], lat[:, kc]
        v_f, v_o, v_m, v_l = far[:, vc], kv[:, vc], mid[:, vc], lat[:, vc]
        c = scale * math.log2(math.e)
        t_c = jnp.where(tri, dot(k_f, qh, NT), dot(k_o, qh, NT)) * c + bias_c[...]
        t_m = dot(k_m, qh, NT) * c + bias_m[...]
        t_l = dot(k_l, qh, NT) * c + bias_l[...]
        top = jnp.maximum(
            jnp.maximum(jnp.max(t_c, axis=0, keepdims=True), jnp.max(t_m, axis=0, keepdims=True)),
            jnp.max(t_l, axis=0, keepdims=True),
        )
        e_c, e_m, e_l = jnp.exp2(t_c - top), jnp.exp2(t_m - top), jnp.exp2(t_l - top)
        inv = 1.0 / (
            jnp.sum(e_c, axis=0, keepdims=True)
            + jnp.sum(e_m, axis=0, keepdims=True)
            + jnp.sum(e_l, axis=0, keepdims=True)
        )
        p_c, p_m, p_l = e_c * inv, e_m * inv, e_l * inv
        b_c, b_m, b_l = (p.astype(jnp.bfloat16) for p in (p_c, p_m, p_l))
        d_c = jnp.where(tri, dot(v_f, doh, NT), dot(v_o, doh, NT))
        d_m, d_l = dot(v_m, doh, NT), dot(v_l, doh, NT)
        delta = (
            jnp.sum(b_c.astype(jnp.float32) * d_c, axis=0, keepdims=True)
            + jnp.sum(b_m.astype(jnp.float32) * d_m, axis=0, keepdims=True)
            + jnp.sum(b_l.astype(jnp.float32) * d_l, axis=0, keepdims=True)
        )
        g_c = p_c * (d_c - delta)
        g_f = jnp.where(tri, g_c, 0.0).astype(jnp.bfloat16)
        g_o = jnp.where(tri, 0.0, g_c).astype(jnp.bfloat16)
        g_m = (p_m * (d_m - delta)).astype(jnp.bfloat16)
        g_l = (p_l * (d_l - delta)).astype(jnp.bfloat16)
        b_f = jnp.where(tri, p_c, 0.0).astype(jnp.bfloat16)
        b_o = jnp.where(tri, 0.0, p_c).astype(jnp.bfloat16)
        back[:, kc] = (dot(g_f, qh, NN) * scale).astype(jnp.bfloat16)
        back[:, vc] = dot(b_f, doh, NN).astype(jnp.bfloat16)
        near[:, kc] = (dot(g_m, qh, NN) * scale).astype(jnp.bfloat16)
        near[:, vc] = dot(b_m, doh, NN).astype(jnp.bfloat16)
        dkv[:, kc] = (dot(g_o, qh, NN) * scale).astype(jnp.bfloat16)
        dkv[:, vc] = dot(b_o, doh, NN).astype(jnp.bfloat16)
        dlat[:, kc] = dot(g_l, qh, NN) * scale
        dlat[:, vc] = dot(b_l, doh, NN)
        dq_t = dot(k_f, g_f, TN) + dot(k_o, g_o, TN) + dot(k_m, g_m, TN) + dot(k_l, g_l, TN)
        dq[:, kc] = (jnp.transpose(dq_t) * scale).astype(jnp.bfloat16)

    def join_and_send(g):
        for s in (0, 1):
            near_copy(g, s).wait_recv()
            w = cols(g, s)
            back[:, w] = (back[:, w].astype(jnp.float32) + near_in[:, w].astype(jnp.float32)).astype(
                jnp.bfloat16
            )

            @pl.when(has_behind)
            def _(s=s):
                back_copy(g, s).start()

    def give_half(g):
        for s in (0, 1):
            w = cols(g, s)
            half_out[:, w] = dlat[pl.ds(pl.multiple_of((1 - core) * half, 16), half), w].astype(jnp.bfloat16)
            half_copy(g, s).start()

    def take_half(g):
        for s in (0, 1):
            half_copy(g, s).wait_recv()
            w = cols(g, s)
            half_sum[:, w] = (
                dlat[pl.ds(pl.multiple_of(core * half, 16), half), w] + half_in[:, w].astype(jnp.float32)
            ).astype(jnp.bfloat16)
        each_batch = groups // batches

        @pl.when(lax.rem(g + 1, each_batch) == 0)
        def _():
            for s in (0, 1):
                chips_on(lambda i, s=s: term_copy(g // each_batch, s, i).start())

    def group(g, carry):
        @pl.when(has_behind)
        def _():
            for s in (0, 1):
                far_copy(g, s).wait_recv()

        @pl.when(core == 1)
        def _():
            for s in (0, 1):
                mid_copy(far, g, s).start()

        for s in (0, 1):
            mid_copy(kv, g, s).wait_recv()
        for i in range(PER):
            head(g * PER + i)
        for s in (0, 1):
            near_copy(g, s).start()
        if inside:
            give_half(g)

        @pl.when((core == 0) & has_behind)
        def _():
            for s in (0, 1):
                back_copy(g, s).start()

        @pl.when((core == 1) & (g > 0))
        def _():
            join_and_send(g - 1)

        if inside:

            @pl.when(g > 0)
            def _():
                take_half(g - 1)

        return carry

    lax.fori_loop(0, groups, group, 0)

    @pl.when(core == 1)
    def _():
        join_and_send(groups - 1)

    if inside:
        take_half(groups - 1)

    def add_in(ref, g, s):
        w = cols(g, s)
        dkv[:, w] = (dkv[:, w].astype(jnp.float32) + ref[:, w].astype(jnp.float32)).astype(jnp.bfloat16)

    def finish(g, s):
        w = cols(g, s)
        near_copy(g, s).wait_recv()
        back_copy(g, s).wait_recv()
        dkv[:, w] = (
            dkv[:, w].astype(jnp.float32) + near_in[:, w].astype(jnp.float32) + far_in[:, w].astype(jnp.float32)
        ).astype(jnp.bfloat16)

    def finish_odd(g, s):
        back_copy(g, s).wait_recv()
        add_in(far_in, g, s)

    def finish_last(g, s):
        near_copy(g, s).wait_recv()
        add_in(near_in, g, s)

    @pl.when((core == 0) & has_ahead)
    def _():
        each(finish)

    @pl.when((core == 1) & has_ahead)
    def _():
        each(finish_odd)

    @pl.when((core == 0) & jnp.logical_not(has_ahead))
    def _():
        each(finish_last)

    def sent(g, s):
        mid_copy(kv, g, s).wait_send()
        near_copy(g, s).wait_send()

    each(sent)

    if inside:
        mine = pl.ds(pl.multiple_of(chip * own, 16), own)
        terms[mine, :] = half_sum[mine, :]
        for b in range(batches):
            for s in (0, 1):
                chips_on(lambda i, b=b, s=s: term_copy(b, s, i).wait_recv())
        total_lat = terms[0:own, :].astype(jnp.float32)
        for k in range(1, chips):
            total_lat = total_lat + terms[k * own : (k + 1) * own, :].astype(jnp.float32)
        dlat_out[...] = total_lat.astype(jnp.bfloat16)
        swap_copy(0).wait_send()
        chips_on(lambda i: lat_copy(i).wait_send())
        chips_on(lambda i: swap_copy(i).wait_send())
        each(lambda g, s: half_copy(g, s).wait_send())
        for b in range(batches):
            for s in (0, 1):
                chips_on(lambda i, b=b, s=s: term_copy(b, s, i).wait_send())

    @pl.when(has_ahead)
    def _():
        each(lambda g, s: far_copy(g, s).wait_send())

    @pl.when(has_behind)
    def _():
        each(lambda g, s: back_copy(g, s).wait_send())


def shards(query, keys_values, dout, lengths, latent_kv):
    n = lax.axis_size("seq")
    rows, width = query.shape
    groups = width // (PER * DH)
    own = latent_kv.shape[0]
    lats = own * n
    chips = n // 2
    inside = own % 16 == 0 and chips <= 16
    latents = latent_kv if inside else lax.all_gather(latent_kv, "seq", axis=0, tiled=True)
    batches = max(b for b in (1, 2, 3) if groups % b == 0)
    if inside:
        tall = pltpu.VMEM((lats // 2, 2 * width), jnp.bfloat16)
        dma = pltpu.SemaphoreType.DMA
        more = [
            pltpu.VMEM((lats, 2 * width), jnp.bfloat16), pltpu.VMEM((lats, 2 * width), jnp.float32),
            tall, tall, tall, tall,
        ] + [dma((chips,))] * 4 + [dma((groups, 2))] * 2 + [dma((batches, 2, chips))] * 2
        lat_out = jax.ShapeDtypeStruct((own, 2 * width), jnp.bfloat16)
    else:
        more = []
        lat_out = jax.ShapeDtypeStruct((lats, 2 * width), jnp.float32)
    vmem = pl.BlockSpec(memory_space=pltpu.VMEM)
    wide = pltpu.VMEM((rows, 2 * width), jnp.bfloat16)
    sem = pltpu.SemaphoreType.DMA((groups, 2))
    grad_query, grad_kv, terms = pl.pallas_call(
        functools.partial(kernel, n, inside),
        out_shape=(
            jax.ShapeDtypeStruct((rows, width), jnp.bfloat16),
            jax.ShapeDtypeStruct((rows, 2 * width), jnp.bfloat16),
            lat_out,
        ),
        in_specs=[vmem, vmem, vmem, pl.BlockSpec(memory_space=pltpu.SMEM), vmem],
        out_specs=(vmem, vmem, vmem),
        scratch_shapes=[wide] * 6
        + [
            pltpu.VMEM((rows, rows), jnp.float32),
            pltpu.VMEM((rows, rows), jnp.float32),
            pltpu.VMEM((lats, rows), jnp.float32),
        ]
        + [sem] * 8
        + more,
        compiler_params=pltpu.CompilerParams(
            collective_id=0, has_side_effects=True, vmem_limit_bytes=56 << 20
        ),
    )(query, keys_values, dout, lengths, latents)
    if inside:
        return grad_query, grad_kv, terms
    grad_latent = lax.psum_scatter(terms, "seq", scatter_dimension=0, tiled=True)
    return grad_query, grad_kv, grad_latent.astype(jnp.bfloat16)


def solution(mesh):
    split = P(("group", "seq"), None)
    return jax.shard_map(
        shards,
        mesh=mesh,
        in_specs=(split, split, split, P("group"), split),
        out_specs=(split, split, split),
        check_vma=False,
    )
```

```python
import functools
import math

import jax
import jax.numpy as jnp
from jax import lax
from jax.experimental import pallas as pl
from jax.experimental.pallas import tpu as pltpu
from jax.sharding import PartitionSpec as P

DH = 128
MESHES = 4
PER = 1
MESH = pl.DeviceIdType.MESH
NT = (((1,), (1,)), ((), ()))
NN = (((1,), (0,)), ((), ()))
TN = (((0,), (0,)), ((), ()))


def dot(a, b, dims):
    return lax.dot_general(a, b, dims, preferred_element_type=jnp.float32)


def kernel(
    n, inside, q, kv, do, lengths, lat_in, dq, dkv, dlat_out,
    far, mid, back, near, near_in, far_in, bias_c, bias_m, bias_l,
    s_far, r_far, s_mid, r_mid, s_near, r_near, s_back, r_back, *more,
):
    if inside:
        lat, dlat, half_out, half_in, half_sum, terms, side_out, side_in = more[:8]
        s_lat, r_lat, s_swap, r_swap, s_half, r_half, s_term, r_term, s_side, r_side = more[8:]
    else:
        lat, dlat = lat_in, dlat_out
    me = lax.axis_index("seq")
    core = lax.rem(me, 2)
    partner = me + 1 - 2 * core
    ahead, behind = lax.rem(me + 2, n), lax.rem(me + n - 2, n)
    rows, width = q.shape
    lats = lat.shape[0]
    half = lats // 2
    groups = width // (PER * DH)
    scale = 1.0 / math.sqrt(DH)
    has_ahead, has_behind = me + 2 < n, me >= 2

    barrier = pltpu.get_barrier_semaphore()
    chips = n // 2
    chip = me // 2

    pairs = chips // 2
    pair, side = chip // 2, lax.rem(chip, 2)
    across = (pair * 2 + 1 - side) * 2 + core

    def onward(i):
        return (lax.rem(pair + i, pairs) * 2 + side) * 2 + core

    greeted = [partner, ahead, behind]
    if inside:
        greeted = [partner, across] + [onward(i) for i in range(1, pairs)] + [ahead, behind]
    for other in greeted:
        pl.semaphore_signal(barrier, inc=1, device_id={"seq": other}, device_id_type=MESH)
    pl.semaphore_wait(barrier, len(greeted))

    def cols(g, s):
        return pl.ds(pl.multiple_of(s * width + g * (PER * DH), DH), PER * DH)

    def copy(src, dst, send, recv, to, g, s):
        return pltpu.make_async_remote_copy(
            src_ref=src.at[:, cols(g, s)], dst_ref=dst.at[:, cols(g, s)],
            send_sem=send.at[g, s], recv_sem=recv.at[g, s],
            device_id={"seq": to}, device_id_type=MESH,
        )

    def far_copy(g, s):
        return copy(kv, far, s_far, r_far, ahead, g, s)

    def mid_copy(src, g, s):
        return copy(src, mid, s_mid, r_mid, partner, g, s)

    def near_copy(g, s):
        return copy(near, near_in, s_near, r_near, partner, g, s)

    def back_copy(g, s):
        return copy(back, far_in, s_back, r_back, behind, g, s)

    def each(fn):
        def step(g, carry):
            for s in (0, 1):
                fn(g, s)
            return carry

        lax.fori_loop(0, groups, step, 0)

    if inside:
        own = lat_in.shape[0]
        half = chips * own

        def rows_of(c, k):
            return pl.ds(pl.multiple_of(c * half + k * own, 16), own)

        def lat_rows(kind, i):
            at_side = side + kind - 2 * side * kind
            return rows_of(core, lax.rem(pair + pairs - i, pairs) * 2 + at_side)

        def lat_copy(kind, i, to):
            at = lat_rows(kind, 0)
            return pltpu.make_async_remote_copy(
                src_ref=lat_in if kind == 0 else lat.at[at], dst_ref=lat.at[at],
                send_sem=s_lat.at[kind, i], recv_sem=r_lat.at[kind, i],
                device_id={"seq": to}, device_id_type=MESH,
            )

        def swap_copy(kind, i):
            at = lat_rows(kind, i)
            return pltpu.make_async_remote_copy(
                src_ref=lat_in if (kind, i) == (0, 0) else lat.at[at], dst_ref=lat.at[at],
                send_sem=s_swap.at[kind, i], recv_sem=r_swap.at[kind, i],
                device_id={"seq": partner}, device_id_type=MESH,
            )

        def half_copy(g, s):
            return copy(half_out, half_in, s_half, r_half, partner, g, s)

        batches = s_term.shape[0]
        span = width // batches

        def term_cols(b, s):
            return pl.ds(pl.multiple_of(s * width + b * span, DH), span)

        def term_copy(b, s, i):
            w = term_cols(b, s)
            to = pl.ds(pl.multiple_of(lax.rem(pair + i, pairs) * 2 * own, 16), 2 * own)
            slot = pl.ds(pl.multiple_of(pair * 2 * own, 16), 2 * own)
            return pltpu.make_async_remote_copy(
                src_ref=half_sum.at[to, w], dst_ref=terms.at[slot, w],
                send_sem=s_term.at[b, s, i], recv_sem=r_term.at[b, s, i],
                device_id={"seq": onward(i)}, device_id_type=MESH,
            )

        def side_copy(b, s):
            w = term_cols(b, s)
            return pltpu.make_async_remote_copy(
                src_ref=side_out.at[:, w], dst_ref=side_in.at[:, w],
                send_sem=s_side.at[b, s], recv_sem=r_side.at[b, s],
                device_id={"seq": across}, device_id_type=MESH,
            )

        def pairs_on(fn):
            for i in range(1, pairs):
                fn(i)

        lat_copy(0, 0, across).start()
        pairs_on(lambda i: lat_copy(0, i, onward(i)).start())
        swap_copy(0, 0).start()
        lat[rows_of(core, chip), :] = lat_in[...]

    @pl.when(has_ahead)
    def _():
        each(lambda g, s: far_copy(g, s).start())

    @pl.when(core == 0)
    def _():
        each(lambda g, s: mid_copy(kv, g, s).start())

    @pl.when(jnp.logical_not(has_behind))
    def _():
        far[...] = jnp.zeros_like(far)

    ends = []
    total = jnp.int32(0)
    for k in range(MESHES):
        total = total + lengths[k]
        ends.append(total)

    def seg(pos):
        out = jnp.zeros(pos.shape, jnp.int32)
        for e in ends:
            out = out + jnp.where(pos >= e, 1, 0)
        return out

    key = lax.broadcasted_iota(jnp.int32, (rows, rows), 0)
    qry = lax.broadcasted_iota(jnp.int32, (rows, rows), 1)
    q_seg = seg(me * rows + qry)
    pos_c = me * rows + key - jnp.where(key > qry, 2 * rows, 0)
    bias_c[...] = jnp.where((seg(pos_c) == q_seg) & (pos_c >= 0), 0.0, -1e30)
    pos_m = (me - 1) * rows + key
    bias_m[...] = jnp.where((seg(pos_m) == q_seg) & (pos_m >= 0), 0.0, -1e30)
    l_key = lax.broadcasted_iota(jnp.int32, (lats, rows), 0)
    l_qry = lax.broadcasted_iota(jnp.int32, (lats, rows), 1)
    bias_l[...] = jnp.where(lax.rem(l_key, MESHES) == seg(me * rows + l_qry), 0.0, -1e30)

    if inside:

        lat_copy(0, 0, across).wait_recv()
        pairs_on(lambda i: lat_copy(1, i, onward(i)).start())
        swap_copy(1, 0).start()
        for kind in (0, 1):
            for i in range(1, pairs):
                lat_copy(kind, i, onward(i)).wait_recv()
                swap_copy(kind, i).start()
        for kind in (0, 1):
            for i in range(pairs):
                swap_copy(kind, i).wait_recv()

    def head(h):
        kc = pl.ds(pl.multiple_of(h * DH, DH), DH)
        vc = pl.ds(pl.multiple_of(width + h * DH, DH), DH)
        tri = lax.broadcasted_iota(jnp.int32, (rows, rows), 0) > lax.broadcasted_iota(
            jnp.int32, (rows, rows), 1
        )
        qh, doh = q[:, kc], do[:, kc]
        k_f, k_o, k_m, k_l = far[:, kc], kv[:, kc], mid[:, kc], lat[:, kc]
        v_f, v_o, v_m, v_l = far[:, vc], kv[:, vc], mid[:, vc], lat[:, vc]
        c = scale * math.log2(math.e)
        t_c = jnp.where(tri, dot(k_f, qh, NT), dot(k_o, qh, NT)) * c + bias_c[...]
        t_m = dot(k_m, qh, NT) * c + bias_m[...]
        t_l = dot(k_l, qh, NT) * c + bias_l[...]
        top = jnp.maximum(
            jnp.maximum(jnp.max(t_c, axis=0, keepdims=True), jnp.max(t_m, axis=0, keepdims=True)),
            jnp.max(t_l, axis=0, keepdims=True),
        )
        e_c, e_m, e_l = jnp.exp2(t_c - top), jnp.exp2(t_m - top), jnp.exp2(t_l - top)
        inv = 1.0 / (
            jnp.sum(e_c, axis=0, keepdims=True)
            + jnp.sum(e_m, axis=0, keepdims=True)
            + jnp.sum(e_l, axis=0, keepdims=True)
        )
        p_c, p_m, p_l = e_c * inv, e_m * inv, e_l * inv
        b_c, b_m, b_l = (p.astype(jnp.bfloat16) for p in (p_c, p_m, p_l))
        d_c = jnp.where(tri, dot(v_f, doh, NT), dot(v_o, doh, NT))
        d_m, d_l = dot(v_m, doh, NT), dot(v_l, doh, NT)
        delta = (
            jnp.sum(b_c.astype(jnp.float32) * d_c, axis=0, keepdims=True)
            + jnp.sum(b_m.astype(jnp.float32) * d_m, axis=0, keepdims=True)
            + jnp.sum(b_l.astype(jnp.float32) * d_l, axis=0, keepdims=True)
        )
        g_c = p_c * (d_c - delta)
        g_f = jnp.where(tri, g_c, 0.0).astype(jnp.bfloat16)
        g_o = jnp.where(tri, 0.0, g_c).astype(jnp.bfloat16)
        g_m = (p_m * (d_m - delta)).astype(jnp.bfloat16)
        g_l = (p_l * (d_l - delta)).astype(jnp.bfloat16)
        b_f = jnp.where(tri, p_c, 0.0).astype(jnp.bfloat16)
        b_o = jnp.where(tri, 0.0, p_c).astype(jnp.bfloat16)
        back[:, kc] = (dot(g_f, qh, NN) * scale).astype(jnp.bfloat16)
        back[:, vc] = dot(b_f, doh, NN).astype(jnp.bfloat16)
        near[:, kc] = (dot(g_m, qh, NN) * scale).astype(jnp.bfloat16)
        near[:, vc] = dot(b_m, doh, NN).astype(jnp.bfloat16)
        dkv[:, kc] = (dot(g_o, qh, NN) * scale).astype(jnp.bfloat16)
        dkv[:, vc] = dot(b_o, doh, NN).astype(jnp.bfloat16)
        dlat[:, kc] = dot(g_l, qh, NN) * scale
        dlat[:, vc] = dot(b_l, doh, NN)
        dq_t = dot(k_f, g_f, TN) + dot(k_o, g_o, TN) + dot(k_m, g_m, TN) + dot(k_l, g_l, TN)
        dq[:, kc] = (jnp.transpose(dq_t) * scale).astype(jnp.bfloat16)

    def join_and_send(g):
        for s in (0, 1):
            near_copy(g, s).wait_recv()
            w = cols(g, s)
            back[:, w] = (back[:, w].astype(jnp.float32) + near_in[:, w].astype(jnp.float32)).astype(
                jnp.bfloat16
            )

            @pl.when(has_behind)
            def _(s=s):
                back_copy(g, s).start()

    def give_half(g):
        for s in (0, 1):
            w = cols(g, s)
            half_out[:, w] = dlat[pl.ds(pl.multiple_of((1 - core) * half, 16), half), w].astype(jnp.bfloat16)
            half_copy(g, s).start()

    def take_half(g):
        for s in (0, 1):
            half_copy(g, s).wait_recv()
            w = cols(g, s)
            half_sum[:, w] = (
                dlat[pl.ds(pl.multiple_of(core * half, 16), half), w] + half_in[:, w].astype(jnp.float32)
            ).astype(jnp.bfloat16)
        each_batch = groups // batches

        @pl.when(lax.rem(g + 1, each_batch) == 0)
        def _():
            for s in (0, 1):
                pairs_on(lambda i, s=s: term_copy(g // each_batch, s, i).start())

    def group(g, carry):
        @pl.when(has_behind)
        def _():
            for s in (0, 1):
                far_copy(g, s).wait_recv()

        @pl.when(core == 1)
        def _():
            for s in (0, 1):
                mid_copy(far, g, s).start()

        for s in (0, 1):
            mid_copy(kv, g, s).wait_recv()
        for i in range(PER):
            head(g * PER + i)
        for s in (0, 1):
            near_copy(g, s).start()
        if inside:
            give_half(g)

        @pl.when((core == 0) & has_behind)
        def _():
            for s in (0, 1):
                back_copy(g, s).start()

        @pl.when((core == 1) & (g > 0))
        def _():
            join_and_send(g - 1)

        if inside:

            @pl.when(g > 0)
            def _():
                take_half(g - 1)

        return carry

    lax.fori_loop(0, groups, group, 0)

    @pl.when(core == 1)
    def _():
        join_and_send(groups - 1)

    if inside:
        take_half(groups - 1)
        mine = pl.ds(pl.multiple_of(pair * 2 * own, 16), 2 * own)
        terms[mine, :] = half_sum[mine, :]

        def sum_terms(b, s, at_side):
            w = term_cols(b, s)
            out = jnp.zeros((own, span), jnp.float32)
            for k in range(pairs):
                at = pl.ds(pl.multiple_of(k * 2 * own + at_side * own, 16), own)
                out = out + terms[at, w].astype(jnp.float32)
            return out

        for b in range(batches):
            for s in (0, 1):
                pairs_on(lambda i, b=b, s=s: term_copy(b, s, i).wait_recv())
                side_out[:, term_cols(b, s)] = sum_terms(b, s, 1 - side).astype(jnp.bfloat16)
                side_copy(b, s).start()

    def add_in(ref, g, s):
        w = cols(g, s)
        dkv[:, w] = (dkv[:, w].astype(jnp.float32) + ref[:, w].astype(jnp.float32)).astype(jnp.bfloat16)

    def finish(g, s):
        w = cols(g, s)
        near_copy(g, s).wait_recv()
        back_copy(g, s).wait_recv()
        dkv[:, w] = (
            dkv[:, w].astype(jnp.float32) + near_in[:, w].astype(jnp.float32) + far_in[:, w].astype(jnp.float32)
        ).astype(jnp.bfloat16)

    def finish_odd(g, s):
        back_copy(g, s).wait_recv()
        add_in(far_in, g, s)

    def finish_last(g, s):
        near_copy(g, s).wait_recv()
        add_in(near_in, g, s)

    @pl.when((core == 0) & has_ahead)
    def _():
        each(finish)

    @pl.when((core == 1) & has_ahead)
    def _():
        each(finish_odd)

    @pl.when((core == 0) & jnp.logical_not(has_ahead))
    def _():
        each(finish_last)

    def sent(g, s):
        mid_copy(kv, g, s).wait_send()
        near_copy(g, s).wait_send()

    each(sent)

    if inside:
        for b in range(batches):
            for s in (0, 1):
                side_copy(b, s).wait_recv()
                w = term_cols(b, s)
                dlat_out[:, w] = (sum_terms(b, s, side) + side_in[:, w].astype(jnp.float32)).astype(
                    jnp.bfloat16
                )
        lat_copy(0, 0, across).wait_send()
        for kind in (0, 1):
            pairs_on(lambda i, kind=kind: lat_copy(kind, i, onward(i)).wait_send())
            for i in range(pairs):
                swap_copy(kind, i).wait_send()
        each(lambda g, s: half_copy(g, s).wait_send())
        for b in range(batches):
            for s in (0, 1):
                pairs_on(lambda i, b=b, s=s: term_copy(b, s, i).wait_send())
                side_copy(b, s).wait_send()

    @pl.when(has_ahead)
    def _():
        each(lambda g, s: far_copy(g, s).wait_send())

    @pl.when(has_behind)
    def _():
        each(lambda g, s: back_copy(g, s).wait_send())


def shards(query, keys_values, dout, lengths, latent_kv):
    n = lax.axis_size("seq")
    rows, width = query.shape
    groups = width // (PER * DH)
    own = latent_kv.shape[0]
    lats = own * n
    chips = n // 2
    pairs = chips // 2
    inside = own % 16 == 0 and n % 4 == 0 and 2 <= pairs <= 8
    latents = latent_kv if inside else lax.all_gather(latent_kv, "seq", axis=0, tiled=True)
    batches = max(b for b in (1, 2, 3, 4) if groups % b == 0)
    if inside:
        tall = pltpu.VMEM((lats // 2, 2 * width), jnp.bfloat16)
        low = pltpu.VMEM((own, 2 * width), jnp.bfloat16)
        dma = pltpu.SemaphoreType.DMA
        more = [
            pltpu.VMEM((lats, 2 * width), jnp.bfloat16), pltpu.VMEM((lats, 2 * width), jnp.float32),
            tall, tall, tall, tall, low, low,
        ] + [dma((2, pairs))] * 4 + [dma((groups, 2))] * 2 + [dma((batches, 2, pairs))] * 2 + [dma((batches, 2))] * 2
        lat_out = jax.ShapeDtypeStruct((own, 2 * width), jnp.bfloat16)
    else:
        more = []
        lat_out = jax.ShapeDtypeStruct((lats, 2 * width), jnp.float32)
    vmem = pl.BlockSpec(memory_space=pltpu.VMEM)
    wide = pltpu.VMEM((rows, 2 * width), jnp.bfloat16)
    sem = pltpu.SemaphoreType.DMA((groups, 2))
    grad_query, grad_kv, terms = pl.pallas_call(
        functools.partial(kernel, n, inside),
        out_shape=(
            jax.ShapeDtypeStruct((rows, width), jnp.bfloat16),
            jax.ShapeDtypeStruct((rows, 2 * width), jnp.bfloat16),
            lat_out,
        ),
        in_specs=[vmem, vmem, vmem, pl.BlockSpec(memory_space=pltpu.SMEM), vmem],
        out_specs=(vmem, vmem, vmem),
        scratch_shapes=[wide] * 6
        + [
            pltpu.VMEM((rows, rows), jnp.float32),
            pltpu.VMEM((rows, rows), jnp.float32),
            pltpu.VMEM((lats, rows), jnp.float32),
        ]
        + [sem] * 8
        + more,
        compiler_params=pltpu.CompilerParams(
            collective_id=0, has_side_effects=True, vmem_limit_bytes=56 << 20
        ),
    )(query, keys_values, dout, lengths, latents)
    if inside:
        return grad_query, grad_kv, terms
    grad_latent = lax.psum_scatter(terms, "seq", scatter_dimension=0, tiled=True)
    return grad_query, grad_kv, grad_latent.astype(jnp.bfloat16)


def solution(mesh):
    split = P(("group", "seq"), None)
    return jax.shard_map(
        shards,
        mesh=mesh,
        in_specs=(split, split, split, P("group"), split),
        out_specs=(split, split, split),
        check_vma=False,
    )
```

```python
import functools
import math

import jax
import jax.numpy as jnp
from jax import lax
from jax.experimental import pallas as pl
from jax.experimental.pallas import tpu as pltpu
from jax.sharding import PartitionSpec as P

DH = 128
MESHES = 4
PER = 1
MESH = pl.DeviceIdType.MESH
NT = (((1,), (1,)), ((), ()))
NN = (((1,), (0,)), ((), ()))
TN = (((0,), (0,)), ((), ()))


def dot(a, b, dims):
    return lax.dot_general(a, b, dims, preferred_element_type=jnp.float32)


def kernel(
    n, inside, q, kv, do, lengths, lat_in, dq, dkv, dlat_out,
    far, mid, back, near, near_in, far_in, bias_c, bias_m, bias_l,
    s_far, r_far, s_mid, r_mid, s_near, r_near, s_back, r_back, *more,
):
    if inside:
        lat, dlat, half_out, half_in, half_sum, terms, side_out, side_in = more[:8]
        s_lat, r_lat, s_swap, r_swap, s_half, r_half, s_term, r_term, s_side, r_side = more[8:]
    else:
        lat, dlat = lat_in, dlat_out
    me = lax.axis_index("seq")
    core = lax.rem(me, 2)
    partner = me + 1 - 2 * core
    ahead, behind = lax.rem(me + 2, n), lax.rem(me + n - 2, n)
    rows, width = q.shape
    lats = lat.shape[0]
    half = lats // 2
    groups = width // (PER * DH)
    scale = 1.0 / math.sqrt(DH)
    has_ahead, has_behind = me + 2 < n, me >= 2

    barrier = pltpu.get_barrier_semaphore()
    chips = n // 2
    chip = me // 2

    pairs = chips // 2
    pair, side = chip // 2, lax.rem(chip, 2)
    across = (pair * 2 + 1 - side) * 2 + core

    def onward(i):
        return (lax.rem(pair + i, pairs) * 2 + side) * 2 + core

    greeted = [partner, ahead, behind]
    if inside:
        greeted = [partner, across] + [onward(i) for i in range(1, pairs)] + [ahead, behind]
    for other in greeted:
        pl.semaphore_signal(barrier, inc=1, device_id={"seq": other}, device_id_type=MESH)
    pl.semaphore_wait(barrier, len(greeted))

    def cols(g, s):
        return pl.ds(pl.multiple_of(s * width + g * (PER * DH), DH), PER * DH)

    def copy(src, dst, send, recv, to, g, s):
        return pltpu.make_async_remote_copy(
            src_ref=src.at[:, cols(g, s)], dst_ref=dst.at[:, cols(g, s)],
            send_sem=send.at[g, s], recv_sem=recv.at[g, s],
            device_id={"seq": to}, device_id_type=MESH,
        )

    def far_copy(g, s):
        return copy(kv, far, s_far, r_far, ahead, g, s)

    def mid_copy(src, g, s):
        return copy(src, mid, s_mid, r_mid, partner, g, s)

    def near_copy(g, s):
        return copy(near, near_in, s_near, r_near, partner, g, s)

    def back_copy(g, s):
        return copy(back, far_in, s_back, r_back, behind, g, s)

    def each(fn):
        def step(g, carry):
            for s in (0, 1):
                fn(g, s)
            return carry

        lax.fori_loop(0, groups, step, 0)

    if inside:
        own = lat_in.shape[0]
        half = chips * own

        def rows_of(c, k):
            return pl.ds(pl.multiple_of(c * half + k * own, 16), own)

        def lat_rows(kind, i):
            at_side = side + kind - 2 * side * kind
            return rows_of(core, lax.rem(pair + pairs - i, pairs) * 2 + at_side)

        def lat_copy(kind, i, to):
            at = lat_rows(kind, 0)
            return pltpu.make_async_remote_copy(
                src_ref=lat_in if kind == 0 else lat.at[at], dst_ref=lat.at[at],
                send_sem=s_lat.at[kind, i], recv_sem=r_lat.at[kind, i],
                device_id={"seq": to}, device_id_type=MESH,
            )

        def swap_copy(kind, i):
            at = lat_rows(kind, i)
            return pltpu.make_async_remote_copy(
                src_ref=lat_in if (kind, i) == (0, 0) else lat.at[at], dst_ref=lat.at[at],
                send_sem=s_swap.at[kind, i], recv_sem=r_swap.at[kind, i],
                device_id={"seq": partner}, device_id_type=MESH,
            )

        def half_copy(g, s):
            return copy(half_out, half_in, s_half, r_half, partner, g, s)

        batches = s_term.shape[0]
        span = width // batches

        def term_cols(b, s):
            return pl.ds(pl.multiple_of(s * width + b * span, DH), span)

        def term_copy(b, s, i):
            w = term_cols(b, s)
            to = pl.ds(pl.multiple_of(lax.rem(pair + i, pairs) * 2 * own, 16), 2 * own)
            slot = pl.ds(pl.multiple_of(pair * 2 * own, 16), 2 * own)
            return pltpu.make_async_remote_copy(
                src_ref=half_sum.at[to, w], dst_ref=terms.at[slot, w],
                send_sem=s_term.at[b, s, i], recv_sem=r_term.at[b, s, i],
                device_id={"seq": onward(i)}, device_id_type=MESH,
            )

        def side_copy(b, s):
            w = term_cols(b, s)
            return pltpu.make_async_remote_copy(
                src_ref=side_out.at[:, w], dst_ref=side_in.at[:, w],
                send_sem=s_side.at[b, s], recv_sem=r_side.at[b, s],
                device_id={"seq": across}, device_id_type=MESH,
            )

        def pairs_on(fn):
            for i in range(1, pairs):
                fn(i)

        lat_copy(0, 0, across).start()
        pairs_on(lambda i: lat_copy(0, i, onward(i)).start())
        swap_copy(0, 0).start()
        lat[rows_of(core, chip), :] = lat_in[...]

    @pl.when(has_ahead)
    def _():
        each(lambda g, s: far_copy(g, s).start())

    @pl.when(core == 0)
    def _():
        each(lambda g, s: mid_copy(kv, g, s).start())

    @pl.when(jnp.logical_not(has_behind))
    def _():
        far[...] = jnp.zeros_like(far)

    ends = []
    total = jnp.int32(0)
    for k in range(MESHES):
        total = total + lengths[k]
        ends.append(total)

    def seg(pos):
        out = jnp.zeros(pos.shape, jnp.int32)
        for e in ends:
            out = out + jnp.where(pos >= e, 1, 0)
        return out

    key = lax.broadcasted_iota(jnp.int32, (rows, rows), 0)
    qry = lax.broadcasted_iota(jnp.int32, (rows, rows), 1)
    q_seg = seg(me * rows + qry)
    pos_c = me * rows + key - jnp.where(key > qry, 2 * rows, 0)
    bias_c[...] = jnp.where((seg(pos_c) == q_seg) & (pos_c >= 0), 0.0, -1e30)
    pos_m = (me - 1) * rows + key
    bias_m[...] = jnp.where((seg(pos_m) == q_seg) & (pos_m >= 0), 0.0, -1e30)
    l_key = lax.broadcasted_iota(jnp.int32, (lats, rows), 0)
    l_qry = lax.broadcasted_iota(jnp.int32, (lats, rows), 1)
    bias_l[...] = jnp.where(lax.rem(l_key, MESHES) == seg(me * rows + l_qry), 0.0, -1e30)

    if inside:

        lat_copy(0, 0, across).wait_recv()
        pairs_on(lambda i: lat_copy(1, i, onward(i)).start())
        swap_copy(1, 0).start()
        for kind in (0, 1):
            for i in range(1, pairs):
                lat_copy(kind, i, onward(i)).wait_recv()
                swap_copy(kind, i).start()
        for kind in (0, 1):
            for i in range(pairs):
                swap_copy(kind, i).wait_recv()

    def head(h):
        kc = pl.ds(pl.multiple_of(h * DH, DH), DH)
        vc = pl.ds(pl.multiple_of(width + h * DH, DH), DH)
        tri = lax.broadcasted_iota(jnp.int32, (rows, rows), 0) > lax.broadcasted_iota(
            jnp.int32, (rows, rows), 1
        )
        qh, doh = q[:, kc], do[:, kc]
        k_f, k_o, k_m, k_l = far[:, kc], kv[:, kc], mid[:, kc], lat[:, kc]
        v_f, v_o, v_m, v_l = far[:, vc], kv[:, vc], mid[:, vc], lat[:, vc]
        c = scale * math.log2(math.e)
        t_c = jnp.where(tri, dot(k_f, qh, NT), dot(k_o, qh, NT)) * c + bias_c[...]
        t_m = dot(k_m, qh, NT) * c + bias_m[...]
        t_l = dot(k_l, qh, NT) * c + bias_l[...]
        top = jnp.maximum(
            jnp.maximum(jnp.max(t_c, axis=0, keepdims=True), jnp.max(t_m, axis=0, keepdims=True)),
            jnp.max(t_l, axis=0, keepdims=True),
        )
        e_c, e_m, e_l = jnp.exp2(t_c - top), jnp.exp2(t_m - top), jnp.exp2(t_l - top)
        inv = 1.0 / (
            jnp.sum(e_c, axis=0, keepdims=True)
            + jnp.sum(e_m, axis=0, keepdims=True)
            + jnp.sum(e_l, axis=0, keepdims=True)
        )
        p_c, p_m, p_l = e_c * inv, e_m * inv, e_l * inv
        b_c, b_m, b_l = (p.astype(jnp.bfloat16) for p in (p_c, p_m, p_l))
        d_c = jnp.where(tri, dot(v_f, doh, NT), dot(v_o, doh, NT))
        d_m, d_l = dot(v_m, doh, NT), dot(v_l, doh, NT)
        delta = (
            jnp.sum(b_c.astype(jnp.float32) * d_c, axis=0, keepdims=True)
            + jnp.sum(b_m.astype(jnp.float32) * d_m, axis=0, keepdims=True)
            + jnp.sum(b_l.astype(jnp.float32) * d_l, axis=0, keepdims=True)
        )
        g_c = p_c * (d_c - delta)
        g_f = jnp.where(tri, g_c, 0.0).astype(jnp.bfloat16)
        g_o = jnp.where(tri, 0.0, g_c).astype(jnp.bfloat16)
        g_m = (p_m * (d_m - delta)).astype(jnp.bfloat16)
        g_l = (p_l * (d_l - delta)).astype(jnp.bfloat16)
        b_f = jnp.where(tri, p_c, 0.0).astype(jnp.bfloat16)
        b_o = jnp.where(tri, 0.0, p_c).astype(jnp.bfloat16)
        back[:, kc] = (dot(g_f, qh, NN) * scale).astype(jnp.bfloat16)
        back[:, vc] = dot(b_f, doh, NN).astype(jnp.bfloat16)
        near[:, kc] = (dot(g_m, qh, NN) * scale).astype(jnp.bfloat16)
        near[:, vc] = dot(b_m, doh, NN).astype(jnp.bfloat16)
        dkv[:, kc] = (dot(g_o, qh, NN) * scale).astype(jnp.bfloat16)
        dkv[:, vc] = dot(b_o, doh, NN).astype(jnp.bfloat16)
        dlat[:, kc] = dot(g_l, qh, NN) * scale
        dlat[:, vc] = dot(b_l, doh, NN)
        dq_t = dot(k_f, g_f, TN) + dot(k_o, g_o, TN) + dot(k_m, g_m, TN) + dot(k_l, g_l, TN)
        dq[:, kc] = (jnp.transpose(dq_t) * scale).astype(jnp.bfloat16)

    def join_and_send(g):
        for s in (0, 1):
            near_copy(g, s).wait_recv()
            w = cols(g, s)
            back[:, w] = (back[:, w].astype(jnp.float32) + near_in[:, w].astype(jnp.float32)).astype(
                jnp.bfloat16
            )

            @pl.when(has_behind)
            def _(s=s):
                back_copy(g, s).start()

    def give_half(g):
        for s in (0, 1):
            w = cols(g, s)
            half_out[:, w] = dlat[pl.ds(pl.multiple_of((1 - core) * half, 16), half), w].astype(jnp.bfloat16)
            half_copy(g, s).start()

    def take_half(g):
        for s in (0, 1):
            half_copy(g, s).wait_recv()
            w = cols(g, s)
            half_sum[:, w] = (
                dlat[pl.ds(pl.multiple_of(core * half, 16), half), w] + half_in[:, w].astype(jnp.float32)
            ).astype(jnp.bfloat16)
        each_batch = groups // batches

        @pl.when(lax.rem(g + 1, each_batch) == 0)
        def _():
            for s in (0, 1):
                pairs_on(lambda i, s=s: term_copy(g // each_batch, s, i).start())

    def group(g, carry):
        @pl.when(has_behind)
        def _():
            for s in (0, 1):
                far_copy(g, s).wait_recv()

        @pl.when(core == 1)
        def _():
            for s in (0, 1):
                mid_copy(far, g, s).start()

        @pl.when((core == 1) & (g > 0))
        def _():
            join_and_send(g - 1)

        for s in (0, 1):
            mid_copy(kv, g, s).wait_recv()
        for i in range(PER):
            head(g * PER + i)
        for s in (0, 1):
            near_copy(g, s).start()
        if inside:
            give_half(g)

        @pl.when((core == 0) & has_behind)
        def _():
            for s in (0, 1):
                back_copy(g, s).start()

        if inside:

            @pl.when(g > 0)
            def _():
                take_half(g - 1)

        return carry

    lax.fori_loop(0, groups, group, 0)

    @pl.when(core == 1)
    def _():
        join_and_send(groups - 1)

    if inside:
        take_half(groups - 1)
        mine = pl.ds(pl.multiple_of(pair * 2 * own, 16), 2 * own)
        terms[mine, :] = half_sum[mine, :]

        def sum_terms(b, s, at_side):
            w = term_cols(b, s)
            out = jnp.zeros((own, span), jnp.float32)
            for k in range(pairs):
                at = pl.ds(pl.multiple_of(k * 2 * own + at_side * own, 16), own)
                out = out + terms[at, w].astype(jnp.float32)
            return out

        for b in range(batches):
            for s in (0, 1):
                pairs_on(lambda i, b=b, s=s: term_copy(b, s, i).wait_recv())
                side_out[:, term_cols(b, s)] = sum_terms(b, s, 1 - side).astype(jnp.bfloat16)
                side_copy(b, s).start()

    def add_in(ref, g, s):
        w = cols(g, s)
        dkv[:, w] = (dkv[:, w].astype(jnp.float32) + ref[:, w].astype(jnp.float32)).astype(jnp.bfloat16)

    def finish(g, s):
        w = cols(g, s)
        near_copy(g, s).wait_recv()
        back_copy(g, s).wait_recv()
        dkv[:, w] = (
            dkv[:, w].astype(jnp.float32) + near_in[:, w].astype(jnp.float32) + far_in[:, w].astype(jnp.float32)
        ).astype(jnp.bfloat16)

    def finish_odd(g, s):
        back_copy(g, s).wait_recv()
        add_in(far_in, g, s)

    def finish_last(g, s):
        near_copy(g, s).wait_recv()
        add_in(near_in, g, s)

    @pl.when((core == 0) & has_ahead)
    def _():
        each(finish)

    @pl.when((core == 1) & has_ahead)
    def _():
        each(finish_odd)

    @pl.when((core == 0) & jnp.logical_not(has_ahead))
    def _():
        each(finish_last)

    def sent(g, s):
        mid_copy(kv, g, s).wait_send()
        near_copy(g, s).wait_send()

    each(sent)

    if inside:
        for b in range(batches):
            for s in (0, 1):
                side_copy(b, s).wait_recv()
                w = term_cols(b, s)
                dlat_out[:, w] = (sum_terms(b, s, side) + side_in[:, w].astype(jnp.float32)).astype(
                    jnp.bfloat16
                )
        lat_copy(0, 0, across).wait_send()
        for kind in (0, 1):
            pairs_on(lambda i, kind=kind: lat_copy(kind, i, onward(i)).wait_send())
            for i in range(pairs):
                swap_copy(kind, i).wait_send()
        each(lambda g, s: half_copy(g, s).wait_send())
        for b in range(batches):
            for s in (0, 1):
                pairs_on(lambda i, b=b, s=s: term_copy(b, s, i).wait_send())
                side_copy(b, s).wait_send()

    @pl.when(has_ahead)
    def _():
        each(lambda g, s: far_copy(g, s).wait_send())

    @pl.when(has_behind)
    def _():
        each(lambda g, s: back_copy(g, s).wait_send())


def shards(query, keys_values, dout, lengths, latent_kv):
    n = lax.axis_size("seq")
    rows, width = query.shape
    groups = width // (PER * DH)
    own = latent_kv.shape[0]
    lats = own * n
    chips = n // 2
    pairs = chips // 2
    inside = own % 16 == 0 and n % 4 == 0 and 2 <= pairs <= 8
    latents = latent_kv if inside else lax.all_gather(latent_kv, "seq", axis=0, tiled=True)
    batches = max(b for b in (1, 2, 3, 4) if groups % b == 0)
    if inside:
        tall = pltpu.VMEM((lats // 2, 2 * width), jnp.bfloat16)
        low = pltpu.VMEM((own, 2 * width), jnp.bfloat16)
        dma = pltpu.SemaphoreType.DMA
        more = [
            pltpu.VMEM((lats, 2 * width), jnp.bfloat16), pltpu.VMEM((lats, 2 * width), jnp.float32),
            tall, tall, tall, tall, low, low,
        ] + [dma((2, pairs))] * 4 + [dma((groups, 2))] * 2 + [dma((batches, 2, pairs))] * 2 + [dma((batches, 2))] * 2
        lat_out = jax.ShapeDtypeStruct((own, 2 * width), jnp.bfloat16)
    else:
        more = []
        lat_out = jax.ShapeDtypeStruct((lats, 2 * width), jnp.float32)
    vmem = pl.BlockSpec(memory_space=pltpu.VMEM)
    wide = pltpu.VMEM((rows, 2 * width), jnp.bfloat16)
    sem = pltpu.SemaphoreType.DMA((groups, 2))
    grad_query, grad_kv, terms = pl.pallas_call(
        functools.partial(kernel, n, inside),
        out_shape=(
            jax.ShapeDtypeStruct((rows, width), jnp.bfloat16),
            jax.ShapeDtypeStruct((rows, 2 * width), jnp.bfloat16),
            lat_out,
        ),
        in_specs=[vmem, vmem, vmem, pl.BlockSpec(memory_space=pltpu.SMEM), vmem],
        out_specs=(vmem, vmem, vmem),
        scratch_shapes=[wide] * 6
        + [
            pltpu.VMEM((rows, rows), jnp.float32),
            pltpu.VMEM((rows, rows), jnp.float32),
            pltpu.VMEM((lats, rows), jnp.float32),
        ]
        + [sem] * 8
        + more,
        compiler_params=pltpu.CompilerParams(
            collective_id=0, has_side_effects=True, vmem_limit_bytes=56 << 20
        ),
    )(query, keys_values, dout, lengths, latents)
    if inside:
        return grad_query, grad_kv, terms
    grad_latent = lax.psum_scatter(terms, "seq", scatter_dimension=0, tiled=True)
    return grad_query, grad_kv, grad_latent.astype(jnp.bfloat16)


def solution(mesh):
    split = P(("group", "seq"), None)
    return jax.shard_map(
        shards,
        mesh=mesh,
        in_specs=(split, split, split, P("group"), split),
        out_specs=(split, split, split),
        check_vma=False,
    )
```

```python
import functools
import math

import jax
import jax.numpy as jnp
from jax import lax
from jax.experimental import pallas as pl
from jax.experimental.pallas import tpu as pltpu
from jax.sharding import PartitionSpec as P

DH = 128
MESHES = 4
FLIGHT = 4
PER = 1
MESH = pl.DeviceIdType.MESH
NT = (((1,), (1,)), ((), ()))
NN = (((1,), (0,)), ((), ()))
TN = (((0,), (0,)), ((), ()))


def dot(a, b, dims):
    return lax.dot_general(a, b, dims, preferred_element_type=jnp.float32)


def kernel(
    n, inside, q, kv, do, lengths, lat_in, dq, dkv, dlat_out,
    far, mid, back, near, near_in, far_in, bias_c, bias_m, bias_l,
    s_far, r_far, s_mid, r_mid, s_near, r_near, s_back, r_back, *more,
):
    if inside:
        lat, dlat, half_out, half_in, half_sum, terms, side_out, side_in = more[:8]
        s_lat, r_lat, s_swap, r_swap, s_half, r_half, s_term, r_term, s_side, r_side = more[8:]
    else:
        lat, dlat = lat_in, dlat_out
    me = lax.axis_index("seq")
    core = lax.rem(me, 2)
    partner = me + 1 - 2 * core
    ahead, behind = lax.rem(me + 2, n), lax.rem(me + n - 2, n)
    rows, width = q.shape
    lats = lat.shape[0]
    half = lats // 2
    groups = width // (PER * DH)
    scale = 1.0 / math.sqrt(DH)
    has_ahead, has_behind = me + 2 < n, me >= 2

    barrier = pltpu.get_barrier_semaphore()
    chips = n // 2
    chip = me // 2

    pairs = chips // 2
    pair, side = chip // 2, lax.rem(chip, 2)
    across = (pair * 2 + 1 - side) * 2 + core

    def onward(i):
        return (lax.rem(pair + i, pairs) * 2 + side) * 2 + core

    greeted = [partner, ahead, behind]
    if inside:
        greeted = [partner, across] + [onward(i) for i in range(1, pairs)] + [ahead, behind]
    for other in greeted:
        pl.semaphore_signal(barrier, inc=1, device_id={"seq": other}, device_id_type=MESH)
    pl.semaphore_wait(barrier, len(greeted))

    def cols(g, s):
        return pl.ds(pl.multiple_of(s * width + g * (PER * DH), DH), PER * DH)

    def copy(src, dst, send, recv, to, g, s):
        return pltpu.make_async_remote_copy(
            src_ref=src.at[:, cols(g, s)], dst_ref=dst.at[:, cols(g, s)],
            send_sem=send.at[g, s], recv_sem=recv.at[g, s],
            device_id={"seq": to}, device_id_type=MESH,
        )

    def far_copy(g, s):
        return copy(kv, far, s_far, r_far, ahead, g, s)

    def mid_copy(src, g, s):
        return copy(src, mid, s_mid, r_mid, partner, g, s)

    def near_copy(g, s):
        return copy(near, near_in, s_near, r_near, partner, g, s)

    def back_copy(g, s):
        return copy(back, far_in, s_back, r_back, behind, g, s)

    def each(fn):
        def step(g, carry):
            for s in (0, 1):
                fn(g, s)
            return carry

        lax.fori_loop(0, groups, step, 0)

    if inside:
        own = lat_in.shape[0]
        half = chips * own

        def rows_of(c, k):
            return pl.ds(pl.multiple_of(c * half + k * own, 16), own)

        def lat_rows(kind, i):
            at_side = side + kind - 2 * side * kind
            return rows_of(core, lax.rem(pair + pairs - i, pairs) * 2 + at_side)

        def lat_copy(kind, i, to):
            at = lat_rows(kind, 0)
            return pltpu.make_async_remote_copy(
                src_ref=lat_in if kind == 0 else lat.at[at], dst_ref=lat.at[at],
                send_sem=s_lat.at[kind, i], recv_sem=r_lat.at[kind, i],
                device_id={"seq": to}, device_id_type=MESH,
            )

        def swap_copy(kind, i):
            at = lat_rows(kind, i)
            return pltpu.make_async_remote_copy(
                src_ref=lat_in if (kind, i) == (0, 0) else lat.at[at], dst_ref=lat.at[at],
                send_sem=s_swap.at[kind, i], recv_sem=r_swap.at[kind, i],
                device_id={"seq": partner}, device_id_type=MESH,
            )

        def half_copy(g, s):
            return copy(half_out, half_in, s_half, r_half, partner, g, s)

        batches = s_term.shape[0]
        span = width // batches

        def term_cols(b, s):
            return pl.ds(pl.multiple_of(s * width + b * span, DH), span)

        def term_copy(b, s, i):
            w = term_cols(b, s)
            to = pl.ds(pl.multiple_of(lax.rem(pair + i, pairs) * 2 * own, 16), 2 * own)
            slot = pl.ds(pl.multiple_of(pair * 2 * own, 16), 2 * own)
            return pltpu.make_async_remote_copy(
                src_ref=half_sum.at[to, w], dst_ref=terms.at[slot, w],
                send_sem=s_term.at[b, s, i], recv_sem=r_term.at[b, s, i],
                device_id={"seq": onward(i)}, device_id_type=MESH,
            )

        def side_copy(b, s):
            w = term_cols(b, s)
            return pltpu.make_async_remote_copy(
                src_ref=side_out.at[:, w], dst_ref=side_in.at[:, w],
                send_sem=s_side.at[b, s], recv_sem=r_side.at[b, s],
                device_id={"seq": across}, device_id_type=MESH,
            )

        def pairs_on(fn):
            for i in range(1, pairs):
                fn(i)

        lat_copy(0, 0, across).start()
        pairs_on(lambda i: lat_copy(0, i, onward(i)).start())
        swap_copy(0, 0).start()
        lat[rows_of(core, chip), :] = lat_in[...]

    @pl.when(has_ahead)
    def _():
        for g in range(min(FLIGHT, groups)):
            for s in (0, 1):
                far_copy(g, s).start()

    @pl.when(core == 0)
    def _():
        each(lambda g, s: mid_copy(kv, g, s).start())

    @pl.when(jnp.logical_not(has_behind))
    def _():
        far[...] = jnp.zeros_like(far)

    ends = []
    total = jnp.int32(0)
    for k in range(MESHES):
        total = total + lengths[k]
        ends.append(total)

    def seg(pos):
        out = jnp.zeros(pos.shape, jnp.int32)
        for e in ends:
            out = out + jnp.where(pos >= e, 1, 0)
        return out

    key = lax.broadcasted_iota(jnp.int32, (rows, rows), 0)
    qry = lax.broadcasted_iota(jnp.int32, (rows, rows), 1)
    q_seg = seg(me * rows + qry)
    pos_c = me * rows + key - jnp.where(key > qry, 2 * rows, 0)
    bias_c[...] = jnp.where((seg(pos_c) == q_seg) & (pos_c >= 0), 0.0, -1e30)
    pos_m = (me - 1) * rows + key
    bias_m[...] = jnp.where((seg(pos_m) == q_seg) & (pos_m >= 0), 0.0, -1e30)
    l_key = lax.broadcasted_iota(jnp.int32, (lats, rows), 0)
    l_qry = lax.broadcasted_iota(jnp.int32, (lats, rows), 1)
    bias_l[...] = jnp.where(lax.rem(l_key, MESHES) == seg(me * rows + l_qry), 0.0, -1e30)

    if inside:

        lat_copy(0, 0, across).wait_recv()
        pairs_on(lambda i: lat_copy(1, i, onward(i)).start())
        swap_copy(1, 0).start()
        for kind in (0, 1):
            for i in range(1, pairs):
                lat_copy(kind, i, onward(i)).wait_recv()
                swap_copy(kind, i).start()
        for kind in (0, 1):
            for i in range(pairs):
                swap_copy(kind, i).wait_recv()

    def head(h):
        kc = pl.ds(pl.multiple_of(h * DH, DH), DH)
        vc = pl.ds(pl.multiple_of(width + h * DH, DH), DH)
        tri = lax.broadcasted_iota(jnp.int32, (rows, rows), 0) > lax.broadcasted_iota(
            jnp.int32, (rows, rows), 1
        )
        qh, doh = q[:, kc], do[:, kc]
        k_f, k_o, k_m, k_l = far[:, kc], kv[:, kc], mid[:, kc], lat[:, kc]
        v_f, v_o, v_m, v_l = far[:, vc], kv[:, vc], mid[:, vc], lat[:, vc]
        c = scale * math.log2(math.e)
        t_c = jnp.where(tri, dot(k_f, qh, NT), dot(k_o, qh, NT)) * c + bias_c[...]
        t_m = dot(k_m, qh, NT) * c + bias_m[...]
        t_l = dot(k_l, qh, NT) * c + bias_l[...]
        top = jnp.maximum(
            jnp.maximum(jnp.max(t_c, axis=0, keepdims=True), jnp.max(t_m, axis=0, keepdims=True)),
            jnp.max(t_l, axis=0, keepdims=True),
        )
        e_c, e_m, e_l = jnp.exp2(t_c - top), jnp.exp2(t_m - top), jnp.exp2(t_l - top)
        inv = 1.0 / (
            jnp.sum(e_c, axis=0, keepdims=True)
            + jnp.sum(e_m, axis=0, keepdims=True)
            + jnp.sum(e_l, axis=0, keepdims=True)
        )
        p_c, p_m, p_l = e_c * inv, e_m * inv, e_l * inv
        b_c, b_m, b_l = (p.astype(jnp.bfloat16) for p in (p_c, p_m, p_l))
        d_c = jnp.where(tri, dot(v_f, doh, NT), dot(v_o, doh, NT))
        d_m, d_l = dot(v_m, doh, NT), dot(v_l, doh, NT)
        delta = (
            jnp.sum(b_c.astype(jnp.float32) * d_c, axis=0, keepdims=True)
            + jnp.sum(b_m.astype(jnp.float32) * d_m, axis=0, keepdims=True)
            + jnp.sum(b_l.astype(jnp.float32) * d_l, axis=0, keepdims=True)
        )
        g_c = p_c * (d_c - delta)
        g_f = jnp.where(tri, g_c, 0.0).astype(jnp.bfloat16)
        g_o = jnp.where(tri, 0.0, g_c).astype(jnp.bfloat16)
        g_m = (p_m * (d_m - delta)).astype(jnp.bfloat16)
        g_l = (p_l * (d_l - delta)).astype(jnp.bfloat16)
        b_f = jnp.where(tri, p_c, 0.0).astype(jnp.bfloat16)
        b_o = jnp.where(tri, 0.0, p_c).astype(jnp.bfloat16)
        back[:, kc] = (dot(g_f, qh, NN) * scale).astype(jnp.bfloat16)
        back[:, vc] = dot(b_f, doh, NN).astype(jnp.bfloat16)
        near[:, kc] = (dot(g_m, qh, NN) * scale).astype(jnp.bfloat16)
        near[:, vc] = dot(b_m, doh, NN).astype(jnp.bfloat16)
        dkv[:, kc] = (dot(g_o, qh, NN) * scale).astype(jnp.bfloat16)
        dkv[:, vc] = dot(b_o, doh, NN).astype(jnp.bfloat16)
        dlat[:, kc] = dot(g_l, qh, NN) * scale
        dlat[:, vc] = dot(b_l, doh, NN)
        dq_t = dot(k_f, g_f, TN) + dot(k_o, g_o, TN) + dot(k_m, g_m, TN) + dot(k_l, g_l, TN)
        dq[:, kc] = (jnp.transpose(dq_t) * scale).astype(jnp.bfloat16)

    def join_and_send(g):
        for s in (0, 1):
            near_copy(g, s).wait_recv()
            w = cols(g, s)
            back[:, w] = (back[:, w].astype(jnp.float32) + near_in[:, w].astype(jnp.float32)).astype(
                jnp.bfloat16
            )

            @pl.when(has_behind)
            def _(s=s):
                back_copy(g, s).start()

    def give_half(g):
        for s in (0, 1):
            w = cols(g, s)
            half_out[:, w] = dlat[pl.ds(pl.multiple_of((1 - core) * half, 16), half), w].astype(jnp.bfloat16)
            half_copy(g, s).start()

    def take_half(g):
        for s in (0, 1):
            half_copy(g, s).wait_recv()
            w = cols(g, s)
            half_sum[:, w] = (
                dlat[pl.ds(pl.multiple_of(core * half, 16), half), w] + half_in[:, w].astype(jnp.float32)
            ).astype(jnp.bfloat16)
        each_batch = groups // batches

        @pl.when(lax.rem(g + 1, each_batch) == 0)
        def _():
            for s in (0, 1):
                pairs_on(lambda i, s=s: term_copy(g // each_batch, s, i).start())

    def group(g, carry):
        @pl.when(has_behind)
        def _():
            for s in (0, 1):
                far_copy(g, s).wait_recv()

        @pl.when(has_ahead & (g + FLIGHT < groups))
        def _():
            for s in (0, 1):
                far_copy(g + FLIGHT, s).start()

        @pl.when(core == 1)
        def _():
            for s in (0, 1):
                mid_copy(far, g, s).start()

        @pl.when((core == 1) & (g > 0))
        def _():
            join_and_send(g - 1)

        for s in (0, 1):
            mid_copy(kv, g, s).wait_recv()
        for i in range(PER):
            head(g * PER + i)
        for s in (0, 1):
            near_copy(g, s).start()
        if inside:
            give_half(g)

        @pl.when((core == 0) & has_behind)
        def _():
            for s in (0, 1):
                back_copy(g, s).start()

        if inside:

            @pl.when(g > 0)
            def _():
                take_half(g - 1)

        return carry

    lax.fori_loop(0, groups, group, 0)

    @pl.when(core == 1)
    def _():
        join_and_send(groups - 1)

    if inside:
        take_half(groups - 1)
        mine = pl.ds(pl.multiple_of(pair * 2 * own, 16), 2 * own)
        terms[mine, :] = half_sum[mine, :]

        def sum_terms(b, s, at_side):
            w = term_cols(b, s)
            out = jnp.zeros((own, span), jnp.float32)
            for k in range(pairs):
                at = pl.ds(pl.multiple_of(k * 2 * own + at_side * own, 16), own)
                out = out + terms[at, w].astype(jnp.float32)
            return out

        for b in range(batches):
            for s in (0, 1):
                pairs_on(lambda i, b=b, s=s: term_copy(b, s, i).wait_recv())
                side_out[:, term_cols(b, s)] = sum_terms(b, s, 1 - side).astype(jnp.bfloat16)
                side_copy(b, s).start()

    def add_in(ref, g, s):
        w = cols(g, s)
        dkv[:, w] = (dkv[:, w].astype(jnp.float32) + ref[:, w].astype(jnp.float32)).astype(jnp.bfloat16)

    def finish(g, s):
        w = cols(g, s)
        near_copy(g, s).wait_recv()
        back_copy(g, s).wait_recv()
        dkv[:, w] = (
            dkv[:, w].astype(jnp.float32) + near_in[:, w].astype(jnp.float32) + far_in[:, w].astype(jnp.float32)
        ).astype(jnp.bfloat16)

    def finish_odd(g, s):
        back_copy(g, s).wait_recv()
        add_in(far_in, g, s)

    def finish_last(g, s):
        near_copy(g, s).wait_recv()
        add_in(near_in, g, s)

    @pl.when((core == 0) & has_ahead)
    def _():
        each(finish)

    @pl.when((core == 1) & has_ahead)
    def _():
        each(finish_odd)

    @pl.when((core == 0) & jnp.logical_not(has_ahead))
    def _():
        each(finish_last)

    def sent(g, s):
        mid_copy(kv, g, s).wait_send()
        near_copy(g, s).wait_send()

    each(sent)

    if inside:
        for b in range(batches):
            for s in (0, 1):
                side_copy(b, s).wait_recv()
                w = term_cols(b, s)
                dlat_out[:, w] = (sum_terms(b, s, side) + side_in[:, w].astype(jnp.float32)).astype(
                    jnp.bfloat16
                )
        lat_copy(0, 0, across).wait_send()
        for kind in (0, 1):
            pairs_on(lambda i, kind=kind: lat_copy(kind, i, onward(i)).wait_send())
            for i in range(pairs):
                swap_copy(kind, i).wait_send()
        each(lambda g, s: half_copy(g, s).wait_send())
        for b in range(batches):
            for s in (0, 1):
                pairs_on(lambda i, b=b, s=s: term_copy(b, s, i).wait_send())
                side_copy(b, s).wait_send()

    @pl.when(has_ahead)
    def _():
        each(lambda g, s: far_copy(g, s).wait_send())

    @pl.when(has_behind)
    def _():
        each(lambda g, s: back_copy(g, s).wait_send())


def shards(query, keys_values, dout, lengths, latent_kv):
    n = lax.axis_size("seq")
    rows, width = query.shape
    groups = width // (PER * DH)
    own = latent_kv.shape[0]
    lats = own * n
    chips = n // 2
    pairs = chips // 2
    inside = own % 16 == 0 and n % 4 == 0 and 2 <= pairs <= 8
    latents = latent_kv if inside else lax.all_gather(latent_kv, "seq", axis=0, tiled=True)
    batches = max(b for b in (1, 2, 3, 4) if groups % b == 0)
    if inside:
        tall = pltpu.VMEM((lats // 2, 2 * width), jnp.bfloat16)
        low = pltpu.VMEM((own, 2 * width), jnp.bfloat16)
        dma = pltpu.SemaphoreType.DMA
        more = [
            pltpu.VMEM((lats, 2 * width), jnp.bfloat16), pltpu.VMEM((lats, 2 * width), jnp.float32),
            tall, tall, tall, tall, low, low,
        ] + [dma((2, pairs))] * 4 + [dma((groups, 2))] * 2 + [dma((batches, 2, pairs))] * 2 + [dma((batches, 2))] * 2
        lat_out = jax.ShapeDtypeStruct((own, 2 * width), jnp.bfloat16)
    else:
        more = []
        lat_out = jax.ShapeDtypeStruct((lats, 2 * width), jnp.float32)
    vmem = pl.BlockSpec(memory_space=pltpu.VMEM)
    wide = pltpu.VMEM((rows, 2 * width), jnp.bfloat16)
    sem = pltpu.SemaphoreType.DMA((groups, 2))
    grad_query, grad_kv, terms = pl.pallas_call(
        functools.partial(kernel, n, inside),
        out_shape=(
            jax.ShapeDtypeStruct((rows, width), jnp.bfloat16),
            jax.ShapeDtypeStruct((rows, 2 * width), jnp.bfloat16),
            lat_out,
        ),
        in_specs=[vmem, vmem, vmem, pl.BlockSpec(memory_space=pltpu.SMEM), vmem],
        out_specs=(vmem, vmem, vmem),
        scratch_shapes=[wide] * 6
        + [
            pltpu.VMEM((rows, rows), jnp.float32),
            pltpu.VMEM((rows, rows), jnp.float32),
            pltpu.VMEM((lats, rows), jnp.float32),
        ]
        + [sem] * 8
        + more,
        compiler_params=pltpu.CompilerParams(
            collective_id=0, has_side_effects=True, vmem_limit_bytes=56 << 20
        ),
    )(query, keys_values, dout, lengths, latents)
    if inside:
        return grad_query, grad_kv, terms
    grad_latent = lax.psum_scatter(terms, "seq", scatter_dimension=0, tiled=True)
    return grad_query, grad_kv, grad_latent.astype(jnp.bfloat16)


def solution(mesh):
    split = P(("group", "seq"), None)
    return jax.shard_map(
        shards,
        mesh=mesh,
        in_specs=(split, split, split, P("group"), split),
        out_specs=(split, split, split),
        check_vma=False,
    )
```
